32 devices in a mesh: dp: 2 (over y), tensor: 16 (over z, x, core).
Axes of the slice: x: 2, y: 2, z: 4, core: 2. Of those that a mesh axis runs over, the one named last changes fastest.
Arguments:
- hidden: bfloat16 [16, 256, 1536], P('dp', 'tensor'), may hold values from -24 to 24
- norm_gain: float32 [1536], replicated, may hold values from 0.1 to 1.9
- embedding: bfloat16 [49664, 1536], P('tensor'), may hold values from -2 to 2
- targets: int32 [16, 256], P('dp', 'tensor'), may hold values from 0 to 49154
- lengths: int32 [16], replicated, may hold values from 1 to 256, 2560 in all
- loss_mask: int32 [16, 256], P('dp', 'tensor'), may hold values 0 or 1
- deal_slots: int32 [16], replicated, may hold values from 0 to 15, as said below
Outputs:
- log_prob: float32 [16, 256], P('dp', 'tensor')
- entropy: float32 [16, 256], P('dp', 'tensor')
The draws below stay inside these ranges and needn't reach their ends.
Inputs may be any that keep to these rules, and one draw needn't show every extreme that they name: A permutation; sequence k lies in data group deal_slots[k] // 8, and each data group's sequences go in equal numbers to every data group.
All inputs are finite; a program needn't handle non-finite values. No bound on the sum of `loss_mask` on one device may be relied on, other than what follows from the above.
Results may differ from the reference program's by a relative error of at most 0.012.
The reference program's roundings to bfloat16 on the way (of `normed`) count: a program that leaves them out, or rounds other values in their place, can miss the bound.
Values may be sent and summed in bfloat16 or wider, within the bound.
A program may use at most 128 MiB of HBM per device.

```python
import math
import jax
import jax.numpy as jnp
import numpy as np
from jax import lax

D = 1536
VREAL = 49155
V = 49664
SLOT = 256
SEQ_GROUP = 8
SEQS = 16


def embedding_parts(key):
    base = jax.random.fold_in(key, 11)
    first_key, second_key = jax.random.split(base)
    noise = jnp.clip(jax.random.normal(first_key, (V, D), jnp.float32), -6.0, 6.0)
    scales = jnp.exp(jax.random.uniform(second_key, (V,), jnp.float32, 0.0, math.log(10.0)))
    return (noise, scales)


def draw_embedding(key, part):
    noise, scales = embedding_parts(key)
    return (0.03 * noise * scales[:, None]).astype(jnp.bfloat16)


def draw_hidden(key, part):
    noise = jnp.clip(jax.random.normal(jax.random.fold_in(key, 23), (SEQS, SLOT, D), jnp.float32), -6.0, 6.0)
    return noise.astype(jnp.bfloat16)


def draw_deal_slots(key, part):
    groups = SEQS // SEQ_GROUP
    base = jax.random.fold_in(key, 37)
    group_keys = jax.random.split(jax.random.fold_in(base, 1), groups)
    pattern = jnp.arange(SEQ_GROUP, dtype=jnp.int32) % groups
    destination = jax.vmap(lambda subkey: jax.random.permutation(subkey, pattern))(group_keys).reshape(-1)
    same_group = (destination[:, None] == destination[None, :]).astype(jnp.int32)
    earlier = jnp.sum(jnp.tril(same_group, -1), axis=1)
    slot_keys = jax.random.split(jax.random.fold_in(base, 2), groups)
    shuffles = jax.vmap(lambda subkey: jax.random.permutation(subkey, SEQ_GROUP))(slot_keys).astype(jnp.int32)
    return (destination * SEQ_GROUP + shuffles[destination, earlier]).astype(jnp.int32)


def plant(result, rng, least, high):
    place = [jax.random.randint(jax.random.fold_in(rng, axis), (), 0, length) for axis, length in enumerate(result.shape)]
    widest = result.shape.index(max(result.shape))
    next_to = place[:widest] + [(place[widest] + 1) % result.shape[widest]] + place[widest + 1:]
    return result.at[tuple(place)].set(least).at[tuple(next_to)].set(high)


def rank_bounds(amount, slope):
    loads = [(1 << 20) // math.isqrt(grade ** slope) + 1 for grade in range(1, amount + 1)]
    spread = 1 + sum(loads) // (1 << 30)
    return np.cumsum(np.array([max(1, weight // spread) for weight in loads]))


def ranked(stream_key, dims, count, slope):
    listing = rank_bounds(count, slope)
    ticket = jax.random.randint(jax.random.fold_in(stream_key, 1), dims, 0, int(listing[count - 1]))
    standing = jnp.searchsorted(jnp.asarray(listing, jnp.int32), ticket, side="right")
    return jax.random.permutation(jax.random.fold_in(stream_key, 2), count)[standing].astype(jnp.int32)


def profile(count, total, bound, slope):
    portions = [(1 << 20) // math.isqrt(standing ** slope) + 1 for standing in range(2, count + 1)]
    surplus, given = total - bound - (count - 1), [1] * (count - 1)
    while surplus > 0:
        free = [i for i in range(count - 1) if given[i] < bound]
        whole, remaining = sum([portions[i] for i in free]), surplus
        for i in free:
            extra = min(bound - given[i], max(1, remaining * portions[i] // whole), surplus)
            given[i] = given[i] + extra
            surplus = surplus - extra
    return np.array([bound] + given)


def uneven_parts(rng, count, total, limit, lean):
    if count == 2:
        one = jax.random.randint(rng, (), max(1, total - limit), min(limit, total - 1) + 1)
        return jnp.stack([one, total - one])
    tallies = jnp.asarray(profile(count, total, limit, lean), jnp.int32)
    pairs = (count - 1) // 2
    donor, sink = tallies[1:1 + 2 * pairs:2], tallies[2:2 + 2 * pairs:2]
    slack = jnp.minimum(donor - 1, limit - sink)
    moved = jax.random.randint(jax.random.fold_in(rng, 1), (pairs,), 0, 1 << 20) % (slack + 1)
    tallies = tallies.at[1:1 + 2 * pairs:2].set(donor - moved).at[2:2 + 2 * pairs:2].set(sink + moved)
    return tallies[jax.random.permutation(jax.random.fold_in(rng, 2), count)]


def setup_inputs(seed: int = 0) -> dict:
    splits = jax.random.split(jax.random.key(seed), 8)
    hidden = draw_hidden(jax.random.fold_in(splits[7], 71), 0)
    norm_gain = jnp.clip(1.0 + 0.18 * jax.random.normal(splits[1], (D,), jnp.float32), 0.1, 1.9)
    embedding = draw_embedding(jax.random.fold_in(splits[7], 71), 0)
    targets = plant(ranked(splits[3], (SEQS, SLOT), VREAL, 2), jax.random.fold_in(splits[3], 3), 0, VREAL - 1).astype(jnp.int32)
    lengths = uneven_parts(splits[4], SEQS, SEQS * SLOT * 5 // 8, SLOT, 2).astype(jnp.int32)
    loss_mask = plant((jax.random.randint(splits[5], (SEQS, SLOT), 0, 4) < 3).astype(jnp.int32), jax.random.fold_in(splits[5], 1), 0, 1)
    deal_slots = draw_deal_slots(jax.random.fold_in(splits[7], 71), 0)
    return dict(hidden=hidden, norm_gain=norm_gain, embedding=embedding, targets=targets, lengths=lengths, loss_mask=loss_mask, deal_slots=deal_slots)


def reference(hidden, norm_gain, embedding, targets, lengths, loss_mask, deal_slots):
    source = hidden[deal_slots]

    def per_sequence(inputs):
        rows, wanted, length, marks = inputs
        values = rows.astype(jnp.float32)
        inverse = lax.rsqrt(lax.optimization_barrier(jnp.mean(values * values, axis=1, keepdims=True)) + 1e-05)
        normed = (values * inverse * norm_gain).astype(jnp.bfloat16)
        logits = jnp.dot(normed, embedding.T, preferred_element_type=jnp.float32)
        columns = jnp.arange(V, dtype=jnp.int32)
        usable = columns[None, :] < VREAL
        maximum = lax.optimization_barrier(jnp.max(jnp.where(usable, logits, -jnp.inf), axis=1))
        weights = jnp.where(usable, jnp.exp(logits - maximum[:, None]), 0.0)
        totals = lax.optimization_barrier(jnp.sum(weights, axis=1))
        weighted = lax.optimization_barrier(jnp.sum(weights * jnp.where(usable, logits, 0.0), axis=1))
        log_total = maximum + jnp.log(totals)
        chosen = jnp.take_along_axis(logits, wanted[:, None].astype(jnp.int32), axis=1)[:, 0]
        positions = jnp.arange(SLOT, dtype=jnp.int32)
        scored = (positions < length) & (marks == 1)
        log_prob = jnp.where(scored, chosen - log_total, 0.0)
        entropy = jnp.where(scored, log_total - weighted / totals, 0.0)
        return (log_prob, entropy)
    log_prob, entropy = lax.map(per_sequence, (source, targets, lengths, loss_mask))
    return (log_prob, entropy)
```

```python
import functools

import jax
import jax.numpy as jnp
from jax import lax
from jax.experimental import pallas as pl
from jax.experimental.pallas import tpu as pltpu
from jax.sharding import PartitionSpec as P

VREAL = 49155
MESH = pl.DeviceIdType.MESH


def vocab_tiles(total, want):
    units = -(-total // 16)
    parts = max(1, -(-total // want))
    starts = [16 * (units * i // parts) for i in range(parts)] + [total]
    return [(a, b - a) for a, b in zip(starts[:-1], starts[1:])]


def kernel(
    groups, n, seqs, tiles, low_valid,
    hidden_ref, gain_ref, table_hbm, wanted_ref, order_ref, out_ref,
    rows_buf, table, ids, fresh, stats,
    table_sem, ids_send, ids_recv, right_send, left_send, sib_send, recv, half_recv,
    stat_send, stat_recv,
):
    ring = n // 2
    last = ring // 2
    rows = hidden_ref.shape[0]
    half = rows // 2
    width = rows // seqs
    vocab = table_hbm.shape[0]
    everyone = groups * n
    g = lax.axis_index("dp")
    r = lax.axis_index("tensor")
    c = lax.rem(r, 2)

    def ring_of(rank):
        pair = rank // 2
        z, x = pair // 2, lax.rem(pair, 2)
        return z + x * (ring - 1 - 2 * z)

    def rank_of(place, core):
        x = place // last
        z = place + x * (ring - 1 - 2 * place)
        return 2 * (2 * z + x) + core

    q = ring_of(r)
    right = rank_of(lax.rem(q + 1, ring), c)
    left = rank_of(lax.rem(q + ring - 1, ring), c)
    sibling = rank_of(q, 1 - c)

    load = pltpu.make_async_copy(table_hbm, table, table_sem)
    load.start()

    barrier = pltpu.get_barrier_semaphore()

    def peer(k):
        return {"dp": lax.rem(g + k // n, groups), "tensor": lax.rem(r + lax.rem(k, n), n)}

    def greet(k, carry):
        pl.semaphore_signal(barrier, inc=1, device_id=peer(k), device_id_type=MESH)
        return carry

    lax.fori_loop(1, everyone, greet, 0)

    values = hidden_ref[...].astype(jnp.float32)
    inverse = lax.rsqrt(jnp.mean(values * values, axis=1, keepdims=True) + 1e-05)
    rows_buf[q, c] = (values * inverse * gain_ref[...]).astype(jnp.bfloat16)
    ids[0] = wanted_ref[...]

    pl.semaphore_wait(barrier, everyone - 1)

    def chunk_copy(place, core, send_sem, recv_sem, to, part=None):
        ref = rows_buf.at[place, core]
        if part is not None:
            ref = rows_buf.at[place, core, pl.ds(part * half, half)]
        return pltpu.make_async_remote_copy(
            src_ref=ref, dst_ref=ref, send_sem=send_sem, recv_sem=recv_sem,
            device_id={"dp": g, "tensor": to}, device_id_type=MESH,
        )

    chunk_copy(q, c, right_send.at[0], recv.at[q, c], right).start()
    chunk_copy(q, c, left_send.at[0], recv.at[q, c], left).start()
    chunk_copy(q, c, sib_send.at[0], recv.at[q, c], sibling).start()

    def ids_copy(k):
        return pltpu.make_async_remote_copy(
            src_ref=wanted_ref, dst_ref=ids.at[k], send_sem=ids_send.at[k], recv_sem=ids_recv,
            device_id=peer(k), device_id_type=MESH,
        )

    def send_ids(k, carry):
        ids_copy(k).start()
        return carry

    lax.fori_loop(1, everyone, send_ids, 0)
    others = pl.ds(1, everyone - 1)
    pltpu.make_async_remote_copy(
        src_ref=ids.at[others], dst_ref=ids.at[others], send_sem=ids_send.at[0],
        recv_sem=ids_recv, device_id=peer(1), device_id_type=MESH,
    ).wait_recv()
    load.wait()

    segment = lax.broadcasted_iota(jnp.int32, (1, rows), 1) // width

    def wanted_of(rank):
        line = jnp.zeros((1, rows), jnp.int32)
        for s in range(seqs):
            seq = order_ref[s]
            back = lax.rem(g - seq // seqs + groups, groups)
            where = back * n + lax.rem(r - rank + n, n)
            line = jnp.where(segment == s, ids[where, pl.ds(lax.rem(seq, seqs), 1), :], line)
        return line

    def stat_copy(k, place, core, j):
        rank = rank_of(place, core)
        slot = j * n + lax.rem(rank - r + n, n)
        return pltpu.make_async_remote_copy(
            src_ref=fresh.at[place, core], dst_ref=stats.at[slot],
            send_sem=stat_send.at[k, core, j], recv_sem=stat_recv,
            device_id={"dp": lax.rem(g + j, groups), "tensor": rank}, device_id_type=MESH,
        )

    def block(b, carry):
        step = (b + 1) // 2
        side = lax.rem(b + 1, 2)
        came_l = lax.rem(q - step + ring, ring)
        came_r = lax.rem(q + step, ring)
        spare = right_send.at[0]

        @pl.when((side == 0) & (step < last))
        def _():
            chunk_copy(came_l, c, spare, recv.at[came_l, c], right).wait_recv()

            @pl.when(step < last - 1)
            def _():
                chunk_copy(came_l, c, right_send.at[step], recv.at[came_l, c], right).start()

            @pl.when(step == last - 1)
            def _():
                chunk_copy(came_l, c, right_send.at[step], half_recv.at[0], right, 0).start()

            chunk_copy(came_l, c, sib_send.at[b], recv.at[came_l, c], sibling).start()
            chunk_copy(came_r, c, spare, recv.at[came_r, c], left).wait_recv()

            @pl.when(step < last - 1)
            def _():
                chunk_copy(came_r, c, left_send.at[step], recv.at[came_r, c], left).start()

            @pl.when(step == last - 1)
            def _():
                chunk_copy(came_r, c, left_send.at[step], half_recv.at[1], left, 1).start()

            chunk_copy(came_r, c, sib_send.at[b + 1], recv.at[came_r, c], sibling).start()

        @pl.when(step == last)
        def _():
            chunk_copy(came_l, c, spare, half_recv.at[0], right, 0).wait_recv()
            chunk_copy(came_l, c, spare, half_recv.at[1], left, 1).wait_recv()
            chunk_copy(came_l, c, sib_send.at[b], recv.at[came_l, c], sibling).start()

        place = came_l + side * (came_r - came_l)
        chunk_copy(place, 1 - c, spare, recv.at[place, 1 - c], sibling).wait_recv()

        x = rows_buf[place].reshape(2 * rows, rows_buf.shape[3])
        target = jnp.concatenate([wanted_of(rank_of(place, 0)), wanted_of(rank_of(place, 1))], axis=1)
        target = target - r * vocab
        sub = lax.broadcasted_iota(jnp.int32, (8, 2 * rows), 0)
        peak = total = weighted = chosen = None
        for start, size in tiles:
            logits = lax.dot_general(
                table[pl.ds(start, size), :], x, (((1,), (1,)), ((), ())),
                preferred_element_type=jnp.float32,
            ).reshape(size // 8, 8, 2 * rows)
            line = lax.broadcasted_iota(jnp.int32, logits.shape, 0) * 8 + sub[None]
            if start + size > low_valid:
                logits = jnp.where(line < VREAL - r * vocab - start, logits, -1e30)
            hit = jnp.sum(jnp.where(line == target[None] - start, logits, 0.0), axis=0)
            top = jnp.max(logits, axis=0)
            new = top if peak is None else jnp.maximum(peak, top)
            diff = logits - new[None]
            weights = jnp.exp(diff)
            fresh_total = jnp.sum(weights, axis=0)
            fresh_weighted = jnp.sum(weights * diff, axis=0)
            if peak is None:
                total, weighted, chosen = fresh_total, fresh_weighted, hit
            else:
                move = peak - new
                factor = jnp.exp(move)
                weighted = factor * (weighted + total * move) + fresh_weighted
                total = factor * total + fresh_total
                chosen = chosen + hit
            peak = new
        top = jnp.max(peak, axis=0, keepdims=True)
        move = peak - top
        factor = jnp.exp(move)
        weighted = jnp.sum(factor * (weighted + total * move), axis=0, keepdims=True)
        total = jnp.sum(factor * total, axis=0, keepdims=True)
        chosen = jnp.sum(chosen, axis=0, keepdims=True)
        packed = jnp.concatenate([top, total, weighted, chosen, top, total, weighted, chosen], axis=0)
        fresh[place, 0] = packed[:, :rows]
        fresh[place, 1] = packed[:, rows:]

        for j in range(1, groups):
            stat_copy(b, place, 0, j).start()
            stat_copy(b, place, 1, j).start()

        @pl.when(b > 0)
        def _():
            stat_copy(b, place, 0, 0).start()
            stat_copy(b, place, 1, 0).start()

        @pl.when(b == 0)
        def _():
            stat_copy(b, place, 1 - c, 0).start()
            stats[0] = fresh[place, c]

        return carry

    lax.fori_loop(0, ring, block, 0)

    pltpu.make_async_remote_copy(
        src_ref=stats.at[others], dst_ref=stats.at[others], send_sem=ids_send.at[0],
        recv_sem=stat_recv, device_id=peer(1), device_id_type=MESH,
    ).wait_recv()

    for j in range(groups):
        peak = stats[j * n:(j + 1) * n, 0, :]
        total = stats[j * n:(j + 1) * n, 1, :]
        weighted = stats[j * n:(j + 1) * n, 2, :]
        chosen = jnp.sum(stats[j * n:(j + 1) * n, 3, :], axis=0, keepdims=True)
        top = jnp.max(peak, axis=0, keepdims=True)
        move = peak - top
        factor = jnp.exp(move)
        weighted = jnp.sum(factor * (weighted + total * move), axis=0, keepdims=True)
        total = jnp.sum(factor * total, axis=0, keepdims=True)
        log_total = jnp.log(total)
        out_ref[j] = jnp.concatenate([chosen - top - log_total, log_total - weighted / total], axis=0)

    def drain_ids(k, carry):
        ids_copy(k).wait_send()
        return carry

    lax.fori_loop(1, everyone, drain_ids, 0)

    def drain_ring(s, carry):
        chunk_copy(q, c, right_send.at[s], recv.at[q, c], right).wait_send()
        chunk_copy(q, c, left_send.at[s], recv.at[q, c], left).wait_send()
        return carry

    lax.fori_loop(0, last - 1, drain_ring, 0)
    chunk_copy(q, c, right_send.at[last - 1], recv.at[q, c], right, 0).wait_send()
    chunk_copy(q, c, left_send.at[last - 1], recv.at[q, c], left, 1).wait_send()

    def drain_block(b, carry):
        chunk_copy(q, c, sib_send.at[b], recv.at[q, c], sibling).wait_send()
        for j in range(1, groups):
            stat_copy(b, q, 0, j).wait_send()
            stat_copy(b, q, 1, j).wait_send()
        stat_copy(b, q, 1 - c, 0).wait_send()

        @pl.when(b > 0)
        def _():
            stat_copy(b, q, c, 0).wait_send()

        return carry

    lax.fori_loop(0, ring, drain_block, 0)


def local(groups, n, hidden, norm_gain, embedding, targets, lengths, loss_mask, deal_slots):
    seqs, width, depth = hidden.shape
    rows = seqs * width
    vocab = embedding.shape[0]
    ring = n // 2
    g = lax.axis_index("dp")
    r = lax.axis_index("tensor")
    every = jnp.arange(groups * seqs, dtype=jnp.int32)
    mine = g * seqs + jnp.arange(seqs, dtype=jnp.int32)
    order = jnp.sum(jnp.where(deal_slots[None, :] == mine[:, None], every[None, :], 0), axis=1)
    wanted = jnp.tile(targets, (1, seqs))
    dma = pltpu.SemaphoreType.DMA
    result = pl.pallas_call(
        functools.partial(
            kernel, groups, n, seqs, vocab_tiles(vocab, 528), VREAL - (n - 1) * vocab
        ),
        out_shape=jax.ShapeDtypeStruct((groups, 2, rows), jnp.float32),
        in_specs=[
            pl.BlockSpec(memory_space=pltpu.VMEM),
            pl.BlockSpec(memory_space=pltpu.VMEM),
            pl.BlockSpec(memory_space=pl.ANY),
            pl.BlockSpec(memory_space=pltpu.VMEM),
            pl.BlockSpec(memory_space=pltpu.SMEM),
        ],
        out_specs=pl.BlockSpec(memory_space=pltpu.VMEM),
        scratch_shapes=[
            pltpu.VMEM((ring, 2, rows, depth), jnp.bfloat16),
            pltpu.VMEM((vocab, depth), jnp.bfloat16),
            pltpu.VMEM((groups * n, seqs, rows), jnp.int32),
            pltpu.VMEM((ring, 2, 8, rows), jnp.float32),
            pltpu.VMEM((groups * n, 8, rows), jnp.float32),
            dma,
            dma((groups * n,)),
            dma,
            dma((ring // 2,)),
            dma((ring // 2,)),
            dma((ring,)),
            dma((ring, 2)),
            dma((2,)),
            dma((ring, 2, groups)),
            dma,
        ],
        compiler_params=pltpu.CompilerParams(
            collective_id=0, has_side_effects=True, vmem_limit_bytes=56 * 2**20
        ),
        cost_estimate=pl.CostEstimate(
            flops=2 * n * rows * vocab * depth,
            bytes_accessed=vocab * depth * 2,
            transcendentals=n * rows * vocab,
        ),
        name="ring_score",
    )(hidden.reshape(rows, depth), norm_gain.reshape(1, depth), embedding, wanted, order)
    slots = deal_slots[mine]
    back = lax.rem(g - slots // seqs + groups, groups)
    place = back * seqs + lax.rem(slots, seqs)
    pick = place[:, None] == jnp.arange(groups * seqs, dtype=jnp.int32)[None, :]
    flat = result.reshape(groups, 2, seqs, width).transpose(1, 0, 2, 3).reshape(2, groups * seqs, width)
    moved = jnp.sum(jnp.where(pick[None, :, :, None], flat[:, None], 0.0), axis=2)
    positions = r * width + jnp.arange(width, dtype=jnp.int32)
    scored = (positions[None, :] < lengths[mine][:, None]) & (loss_mask == 1)
    return jnp.where(scored, moved[0], 0.0), jnp.where(scored, moved[1], 0.0)


def solution(mesh):
    placed = (
        P("dp", "tensor", None),
        P(),
        P("tensor", None),
        P("dp", "tensor"),
        P(),
        P("dp", "tensor"),
        P(),
    )
    return jax.shard_map(
        functools.partial(local, mesh.shape["dp"], mesh.shape["tensor"]),
        mesh=mesh,
        in_specs=placed,
        out_specs=(P("dp", "tensor"), P("dp", "tensor")),
        check_vma=False,
    )
```

```python
import functools

import jax
import jax.numpy as jnp
from jax import lax
from jax.experimental import pallas as pl
from jax.experimental.pallas import tpu as pltpu
from jax.sharding import PartitionSpec as P

VREAL = 49155
MESH = pl.DeviceIdType.MESH


def vocab_tiles(total, want):
    units = total // 32
    parts = max(1, total // want)
    starts = [32 * (units * i // parts) for i in range(parts)] + [total]
    return [(a, b - a) for a, b in zip(starts[:-1], starts[1:])]


def kernel(
    groups, n, seqs, tiles, low_valid,
    hidden_ref, gain_ref, table_hbm, wanted_ref, order_ref, out_ref,
    rows_buf, table, ids, fresh, stats, logits,
    table_sem, ids_send, ids_recv, right_send, left_send, sib_send, recv, half_recv,
    stat_send, stat_recv,
):
    ring = n // 2
    last = ring // 2
    rows = hidden_ref.shape[0]
    half = rows // 2
    width = rows // seqs
    vocab = table_hbm.shape[0]
    everyone = groups * n
    g = lax.axis_index("dp")
    r = lax.axis_index("tensor")
    c = lax.rem(r, 2)

    def ring_of(rank):
        pair = rank // 2
        z, x = pair // 2, lax.rem(pair, 2)
        return z + x * (ring - 1 - 2 * z)

    def rank_of(place, core):
        x = place // last
        z = place + x * (ring - 1 - 2 * place)
        return 2 * (2 * z + x) + core

    q = ring_of(r)
    right = rank_of(lax.rem(q + 1, ring), c)
    left = rank_of(lax.rem(q + ring - 1, ring), c)
    sibling = rank_of(q, 1 - c)

    load = pltpu.make_async_copy(table_hbm, table, table_sem)
    load.start()

    barrier = pltpu.get_barrier_semaphore()

    def peer(k):
        return {"dp": lax.rem(g + k // n, groups), "tensor": lax.rem(r + lax.rem(k, n), n)}

    def greet(k, carry):
        pl.semaphore_signal(barrier, inc=1, device_id=peer(k), device_id_type=MESH)
        return carry

    lax.fori_loop(1, everyone, greet, 0)

    values = hidden_ref[...].astype(jnp.float32)
    inverse = lax.rsqrt(jnp.mean(values * values, axis=1, keepdims=True) + 1e-05)
    rows_buf[q, c] = (values * inverse * gain_ref[...][None, :]).astype(jnp.bfloat16)
    ids[0] = wanted_ref[...]

    pl.semaphore_wait(barrier, everyone - 1)

    def chunk_copy(place, core, send_sem, recv_sem, to, part=None):
        ref = rows_buf.at[place, core]
        if part is not None:
            ref = rows_buf.at[place, core, pl.ds(part * half, half)]
        return pltpu.make_async_remote_copy(
            src_ref=ref, dst_ref=ref, send_sem=send_sem, recv_sem=recv_sem,
            device_id={"dp": g, "tensor": to}, device_id_type=MESH,
        )

    chunk_copy(q, c, right_send.at[0], recv.at[q, c], right).start()
    chunk_copy(q, c, left_send.at[0], recv.at[q, c], left).start()
    chunk_copy(q, c, sib_send.at[0], recv.at[q, c], sibling).start()

    def ids_copy(k):
        return pltpu.make_async_remote_copy(
            src_ref=wanted_ref, dst_ref=ids.at[k], send_sem=ids_send.at[k], recv_sem=ids_recv,
            device_id=peer(k), device_id_type=MESH,
        )

    def send_ids(k, carry):
        ids_copy(k).start()
        return carry

    lax.fori_loop(1, everyone, send_ids, 0)
    others = pl.ds(1, everyone - 1)
    pltpu.make_async_remote_copy(
        src_ref=ids.at[others], dst_ref=ids.at[others], send_sem=ids_send.at[0],
        recv_sem=ids_recv, device_id=peer(1), device_id_type=MESH,
    ).wait_recv()
    load.wait()

    segment = lax.broadcasted_iota(jnp.int32, (1, rows), 1) // width

    def wanted_of(rank):
        line = jnp.zeros((1, rows), jnp.int32)
        for s in range(seqs):
            seq = order_ref[s]
            back = lax.rem(g - seq // seqs + groups, groups)
            where = back * n + lax.rem(r - rank + n, n)
            line = jnp.where(segment == s, ids[where, pl.ds(lax.rem(seq, seqs), 1), :], line)
        return line

    def stat_copy(k, place, core, j):
        rank = rank_of(place, core)
        slot = j * n + lax.rem(rank - r + n, n)
        return pltpu.make_async_remote_copy(
            src_ref=fresh.at[place, core], dst_ref=stats.at[slot],
            send_sem=stat_send.at[k, core, j], recv_sem=stat_recv,
            device_id={"dp": lax.rem(g + j, groups), "tensor": rank}, device_id_type=MESH,
        )

    def pass_on(b, step, side):
        ahead = step + 1
        next_l = lax.rem(q - ahead + ring, ring)
        next_r = lax.rem(q + ahead, ring)
        spare = right_send.at[0]

        @pl.when((side == 1) & (ahead < last))
        def _():
            chunk_copy(next_l, c, spare, recv.at[next_l, c], right).wait_recv()

            @pl.when(ahead < last - 1)
            def _():
                chunk_copy(next_l, c, right_send.at[ahead], recv.at[next_l, c], right).start()

            @pl.when(ahead == last - 1)
            def _():
                chunk_copy(next_l, c, right_send.at[ahead], half_recv.at[0], right, 0).start()

            chunk_copy(next_l, c, sib_send.at[b + 1], recv.at[next_l, c], sibling).start()
            chunk_copy(next_r, c, spare, recv.at[next_r, c], left).wait_recv()

            @pl.when(ahead < last - 1)
            def _():
                chunk_copy(next_r, c, left_send.at[ahead], recv.at[next_r, c], left).start()

            @pl.when(ahead == last - 1)
            def _():
                chunk_copy(next_r, c, left_send.at[ahead], half_recv.at[1], left, 1).start()

            chunk_copy(next_r, c, sib_send.at[b + 2], recv.at[next_r, c], sibling).start()

        @pl.when((side == 1) & (ahead == last))
        def _():
            chunk_copy(next_l, c, spare, half_recv.at[0], right, 0).wait_recv()
            chunk_copy(next_l, c, spare, half_recv.at[1], left, 1).wait_recv()
            chunk_copy(next_l, c, sib_send.at[b + 1], recv.at[next_l, c], sibling).start()

    def block(b, carry):
        step = (b + 1) // 2
        side = lax.rem(b + 1, 2)
        came_l = lax.rem(q - step + ring, ring)
        came_r = lax.rem(q + step, ring)
        spare = right_send.at[0]

        place = came_l + side * (came_r - came_l)
        chunk_copy(place, 1 - c, spare, recv.at[place, 1 - c], sibling).wait_recv()

        x = rows_buf[place].reshape(2 * rows, rows_buf.shape[3])
        target = jnp.concatenate([wanted_of(rank_of(place, 0)), wanted_of(rank_of(place, 1))], axis=1)
        sub = lax.broadcasted_iota(jnp.int32, (8, 2 * rows), 0)
        target = target - r * vocab - sub
        limit = VREAL - r * vocab - sub

        def part(t, start, at, size):
            piece = logits[t % 2, pl.ds(at, size), :].reshape(size // 8, 8, 2 * rows)
            line = lax.broadcasted_iota(jnp.int32, piece.shape, 0) * 8 + (start + at)
            if start + tiles[t][1] > low_valid:
                piece = jnp.where(line < limit[None], piece, -1e30)
            return piece, line

        def sweep(size, step_at, state):
            state = lax.fori_loop(
                0, size // 32, lambda i, old: step_at(pl.multiple_of(i * 32, 32), 32, old), state,
                unroll=True,
            )
            return step_at(size - size % 32, size % 32, state) if size % 32 else state

        def add_tile(t, state):
            start, size = tiles[t]
            peak, total, weighted, chosen = state

            def widen(at, many, new):
                return jnp.maximum(new, jnp.max(part(t, start, at, many)[0], axis=0))

            new = sweep(size, widen, peak)
            move = peak - new
            factor = jnp.exp(move)
            weighted = factor * (weighted + total * move)
            total = factor * total

            def add(at, many, old):
                total, weighted, chosen = old
                piece, line = part(t, start, at, many)
                diff = piece - new[None]
                weights = jnp.exp(diff)
                total = total + jnp.sum(weights, axis=0)
                weighted = weighted + jnp.sum(weights * diff, axis=0)
                chosen = chosen + jnp.sum(jnp.where(line == target[None], piece, 0.0), axis=0)
                return total, weighted, chosen

            total, weighted, chosen = sweep(size, add, (total, weighted, chosen))
            return new, total, weighted, chosen

        zero = jnp.zeros((8, 2 * rows), jnp.float32)
        state = (zero - 1e30, zero, zero, zero)
        for t, (start, size) in enumerate(tiles):
            if t == len(tiles) // 2:
                pass_on(b, step, side)
            logits[t % 2, :size, :] = lax.dot_general(
                table[pl.ds(start, size), :], x, (((1,), (1,)), ((), ())),
                preferred_element_type=jnp.float32,
            )
            if t:
                state = add_tile(t - 1, state)
        peak, total, weighted, chosen = add_tile(len(tiles) - 1, state)
        top = jnp.max(peak, axis=0, keepdims=True)
        move = peak - top
        factor = jnp.exp(move)
        weighted = jnp.sum(factor * (weighted + total * move), axis=0, keepdims=True)
        total = jnp.sum(factor * total, axis=0, keepdims=True)
        chosen = jnp.sum(chosen, axis=0, keepdims=True)
        packed = jnp.concatenate([top, total, weighted, chosen, top, total, weighted, chosen], axis=0)
        fresh[place, 0] = packed[:, :rows]
        fresh[place, 1] = packed[:, rows:]

        for j in range(1, groups):
            stat_copy(b, place, 0, j).start()
            stat_copy(b, place, 1, j).start()

        @pl.when(b > 0)
        def _():
            stat_copy(b, place, 0, 0).start()
            stat_copy(b, place, 1, 0).start()

        @pl.when(b == 0)
        def _():
            stat_copy(b, place, 1 - c, 0).start()
            stats[0] = fresh[place, c]

        return carry

    lax.fori_loop(0, ring, block, 0)

    pltpu.make_async_remote_copy(
        src_ref=stats.at[others], dst_ref=stats.at[others], send_sem=ids_send.at[0],
        recv_sem=stat_recv, device_id=peer(1), device_id_type=MESH,
    ).wait_recv()

    for j in range(groups):
        peak = stats[j * n:(j + 1) * n, 0, :]
        total = stats[j * n:(j + 1) * n, 1, :]
        weighted = stats[j * n:(j + 1) * n, 2, :]
        chosen = jnp.sum(stats[j * n:(j + 1) * n, 3, :], axis=0, keepdims=True)
        top = jnp.max(peak, axis=0, keepdims=True)
        move = peak - top
        factor = jnp.exp(move)
        weighted = jnp.sum(factor * (weighted + total * move), axis=0, keepdims=True)
        total = jnp.sum(factor * total, axis=0, keepdims=True)
        log_total = jnp.log(total)
        out_ref[j] = jnp.concatenate([chosen - top - log_total, log_total - weighted / total], axis=0)

    def drain_ids(k, carry):
        ids_copy(k).wait_send()
        return carry

    lax.fori_loop(1, everyone, drain_ids, 0)

    def drain_ring(s, carry):
        chunk_copy(q, c, right_send.at[s], recv.at[q, c], right).wait_send()
        chunk_copy(q, c, left_send.at[s], recv.at[q, c], left).wait_send()
        return carry

    lax.fori_loop(0, last - 1, drain_ring, 0)
    chunk_copy(q, c, right_send.at[last - 1], recv.at[q, c], right, 0).wait_send()
    chunk_copy(q, c, left_send.at[last - 1], recv.at[q, c], left, 1).wait_send()

    def drain_block(b, carry):
        chunk_copy(q, c, sib_send.at[b], recv.at[q, c], sibling).wait_send()
        for j in range(1, groups):
            stat_copy(b, q, 0, j).wait_send()
            stat_copy(b, q, 1, j).wait_send()
        stat_copy(b, q, 1 - c, 0).wait_send()

        @pl.when(b > 0)
        def _():
            stat_copy(b, q, c, 0).wait_send()

        return carry

    lax.fori_loop(0, ring, drain_block, 0)


def local(groups, n, hidden, norm_gain, embedding, targets, lengths, loss_mask, deal_slots):
    seqs, width, depth = hidden.shape
    rows = seqs * width
    vocab = embedding.shape[0]
    ring = n // 2
    g = lax.axis_index("dp")
    r = lax.axis_index("tensor")
    every = jnp.arange(groups * seqs, dtype=jnp.int32)
    mine = g * seqs + jnp.arange(seqs, dtype=jnp.int32)
    order = jnp.sum(jnp.where(deal_slots[None, :] == mine[:, None], every[None, :], 0), axis=1)
    wanted = jnp.concatenate([targets] * seqs, axis=1)
    tiles = vocab_tiles(vocab, 512)
    dma = pltpu.SemaphoreType.DMA
    result = pl.pallas_call(
        functools.partial(
            kernel, groups, n, seqs, tiles, VREAL - (n - 1) * vocab
        ),
        out_shape=jax.ShapeDtypeStruct((groups, 2, rows), jnp.float32),
        in_specs=[
            pl.BlockSpec(memory_space=pltpu.VMEM),
            pl.BlockSpec(memory_space=pltpu.VMEM),
            pl.BlockSpec(memory_space=pl.ANY),
            pl.BlockSpec(memory_space=pltpu.VMEM),
            pl.BlockSpec(memory_space=pltpu.SMEM),
        ],
        out_specs=pl.BlockSpec(memory_space=pltpu.VMEM),
        scratch_shapes=[
            pltpu.VMEM((ring, 2, rows, depth), jnp.bfloat16),
            pltpu.VMEM((vocab, depth), jnp.bfloat16),
            pltpu.VMEM((groups * n, seqs, rows), jnp.int32),
            pltpu.VMEM((ring, 2, 8, rows), jnp.float32),
            pltpu.VMEM((groups * n, 8, rows), jnp.float32),
            pltpu.VMEM((2, max(size for _, size in tiles), 2 * rows), jnp.float32),
            dma,
            dma((groups * n,)),
            dma,
            dma((ring // 2,)),
            dma((ring // 2,)),
            dma((ring,)),
            dma((ring, 2)),
            dma((2,)),
            dma((ring, 2, groups)),
            dma,
        ],
        compiler_params=pltpu.CompilerParams(
            collective_id=0, has_side_effects=True, vmem_limit_bytes=56 * 2**20
        ),
        cost_estimate=pl.CostEstimate(
            flops=2 * n * rows * vocab * depth,
            bytes_accessed=vocab * depth * 2,
            transcendentals=n * rows * vocab,
        ),
        name="ring_score",
    )(hidden.reshape(rows, depth), norm_gain, embedding, wanted, order)
    slots = lax.dynamic_slice_in_dim(deal_slots, g * seqs, seqs)
    back = lax.rem(g - slots // seqs + groups, groups)
    place = back * seqs + lax.rem(slots, seqs)
    pick = place[:, None] == jnp.arange(groups * seqs, dtype=jnp.int32)[None, :]
    flat = result.reshape(groups, 2, seqs, width).transpose(1, 0, 2, 3).reshape(2, groups * seqs, width)
    moved = jnp.sum(jnp.where(pick[None, :, :, None], flat[:, None], 0.0), axis=2)
    positions = r * width + jnp.arange(width, dtype=jnp.int32)
    scored = (positions[None, :] < lax.dynamic_slice_in_dim(lengths, g * seqs, seqs)[:, None]) & (loss_mask == 1)
    return jnp.where(scored, moved[0], 0.0), jnp.where(scored, moved[1], 0.0)


def solution(mesh):
    placed = (
        P("dp", "tensor", None),
        P(),
        P("tensor", None),
        P("dp", "tensor"),
        P(),
        P("dp", "tensor"),
        P(),
    )
    return jax.shard_map(
        functools.partial(local, mesh.shape["dp"], mesh.shape["tensor"]),
        mesh=mesh,
        in_specs=placed,
        out_specs=(P("dp", "tensor"), P("dp", "tensor")),
        check_vma=False,
    )
```

```python
import functools

import jax
import jax.numpy as jnp
from jax import lax
from jax.experimental import pallas as pl
from jax.experimental.pallas import tpu as pltpu
from jax.sharding import PartitionSpec as P

VREAL = 49155
MESH = pl.DeviceIdType.MESH


def vocab_tiles(total, want):
    units = total // 32
    parts = max(1, total // want)
    starts = [32 * (units * i // parts) for i in range(parts)] + [total]
    return [(a, b - a) for a, b in zip(starts[:-1], starts[1:])]


def kernel(
    groups, n, seqs, tiles, low_valid,
    hidden_ref, gain_ref, table_hbm, wanted_ref, order_ref, out_ref,
    rows_buf, table, ids, fresh, stats, logits,
    table_sem, ids_send, ids_recv, right_send, left_send, sib_send, recv, half_recv,
    stat_send, stat_recv,
):
    ring = n // 2
    last = ring // 2
    rows = hidden_ref.shape[0]
    half = rows // 2
    width = rows // seqs
    vocab = table_hbm.shape[0]
    everyone = groups * n
    g = lax.axis_index("dp")
    r = lax.axis_index("tensor")
    c = lax.rem(r, 2)

    def ring_of(rank):
        pair = rank // 2
        z, x = pair // 2, lax.rem(pair, 2)
        return z + x * (ring - 1 - 2 * z)

    def rank_of(place, core):
        x = place // last
        z = place + x * (ring - 1 - 2 * place)
        return 2 * (2 * z + x) + core

    q = ring_of(r)
    right = rank_of(lax.rem(q + 1, ring), c)
    left = rank_of(lax.rem(q + ring - 1, ring), c)
    sibling = rank_of(q, 1 - c)

    load = pltpu.make_async_copy(table_hbm, table, table_sem)
    load.start()

    barrier = pltpu.get_barrier_semaphore()

    def peer(k):
        return {"dp": lax.rem(g + k // n, groups), "tensor": lax.rem(r + lax.rem(k, n), n)}

    def greet(k, carry):
        pl.semaphore_signal(barrier, inc=1, device_id=peer(k), device_id_type=MESH)
        return carry

    lax.fori_loop(1, everyone, greet, 0)

    values = hidden_ref[...].astype(jnp.float32)
    inverse = lax.rsqrt(jnp.mean(values * values, axis=1, keepdims=True) + 1e-05)
    rows_buf[q, c] = (values * inverse * gain_ref[...][None, :]).astype(jnp.bfloat16)
    ids[0] = wanted_ref[...]

    pl.semaphore_wait(barrier, everyone - 1)

    def chunk_copy(place, core, send_sem, recv_sem, to, part=None):
        ref = rows_buf.at[place, core]
        if part is not None:
            ref = rows_buf.at[place, core, pl.ds(part * half, half)]
        return pltpu.make_async_remote_copy(
            src_ref=ref, dst_ref=ref, send_sem=send_sem, recv_sem=recv_sem,
            device_id={"dp": g, "tensor": to}, device_id_type=MESH,
        )

    chunk_copy(q, c, right_send.at[0], recv.at[q, c], right).start()
    chunk_copy(q, c, left_send.at[0], recv.at[q, c], left).start()
    chunk_copy(q, c, sib_send.at[0], recv.at[q, c], sibling).start()

    def ids_copy(k):
        return pltpu.make_async_remote_copy(
            src_ref=wanted_ref, dst_ref=ids.at[k], send_sem=ids_send.at[k], recv_sem=ids_recv,
            device_id=peer(k), device_id_type=MESH,
        )

    def send_ids(k, carry):
        ids_copy(k).start()
        return carry

    lax.fori_loop(1, everyone, send_ids, 0)
    others = pl.ds(1, everyone - 1)
    pltpu.make_async_remote_copy(
        src_ref=ids.at[others], dst_ref=ids.at[others], send_sem=ids_send.at[0],
        recv_sem=ids_recv, device_id=peer(1), device_id_type=MESH,
    ).wait_recv()
    load.wait()

    segment = lax.broadcasted_iota(jnp.int32, (1, rows), 1) // width

    def wanted_of(rank):
        line = jnp.zeros((1, rows), jnp.int32)
        for s in range(seqs):
            seq = order_ref[s]
            back = lax.rem(g - seq // seqs + groups, groups)
            where = back * n + lax.rem(r - rank + n, n)
            line = jnp.where(segment == s, ids[where, pl.ds(lax.rem(seq, seqs), 1), :], line)
        return line

    def stat_copy(k, place, core, j):
        rank = rank_of(place, core)
        slot = j * n + lax.rem(rank - r + n, n)
        return pltpu.make_async_remote_copy(
            src_ref=fresh.at[place, core], dst_ref=stats.at[slot],
            send_sem=stat_send.at[k, core, j], recv_sem=stat_recv,
            device_id={"dp": lax.rem(g + j, groups), "tensor": rank}, device_id_type=MESH,
        )

    def pass_on(b, step, side):
        ahead = step + 1
        next_l = lax.rem(q - ahead + ring, ring)
        next_r = lax.rem(q + ahead, ring)
        spare = right_send.at[0]

        @pl.when((side == 1) & (ahead < last))
        def _():
            chunk_copy(next_l, c, spare, recv.at[next_l, c], right).wait_recv()

            @pl.when(ahead < last - 1)
            def _():
                chunk_copy(next_l, c, right_send.at[ahead], recv.at[next_l, c], right).start()

            @pl.when(ahead == last - 1)
            def _():
                chunk_copy(next_l, c, right_send.at[ahead], half_recv.at[0], right, 0).start()

            chunk_copy(next_l, c, sib_send.at[b + 1], recv.at[next_l, c], sibling).start()
            chunk_copy(next_r, c, spare, recv.at[next_r, c], left).wait_recv()

            @pl.when(ahead < last - 1)
            def _():
                chunk_copy(next_r, c, left_send.at[ahead], recv.at[next_r, c], left).start()

            @pl.when(ahead == last - 1)
            def _():
                chunk_copy(next_r, c, left_send.at[ahead], half_recv.at[1], left, 1).start()

            chunk_copy(next_r, c, sib_send.at[b + 2], recv.at[next_r, c], sibling).start()

        @pl.when((side == 1) & (ahead == last))
        def _():
            chunk_copy(next_l, c, spare, half_recv.at[0], right, 0).wait_recv()
            chunk_copy(next_l, c, spare, half_recv.at[1], left, 1).wait_recv()
            chunk_copy(next_l, c, sib_send.at[b + 1], recv.at[next_l, c], sibling).start()

    def block(b, carry):
        step = (b + 1) // 2
        side = lax.rem(b + 1, 2)
        came_l = lax.rem(q - step + ring, ring)
        came_r = lax.rem(q + step, ring)
        spare = right_send.at[0]

        place = came_l + side * (came_r - came_l)
        chunk_copy(place, 1 - c, spare, recv.at[place, 1 - c], sibling).wait_recv()

        x = rows_buf[place].reshape(2 * rows, rows_buf.shape[3]).T
        target = jnp.concatenate([wanted_of(rank_of(place, 0)), wanted_of(rank_of(place, 1))], axis=1)
        sub = lax.broadcasted_iota(jnp.int32, (8, 2 * rows), 0)
        target = target - r * vocab - sub
        limit = VREAL - r * vocab - sub

        def part(t, start, at, size):
            piece = logits[t % 2, pl.ds(at, size), :].reshape(size // 8, 8, 2 * rows)
            line = lax.broadcasted_iota(jnp.int32, piece.shape, 0) * 8 + (start + at)
            if start + tiles[t][1] > low_valid:
                piece = jnp.where(line < limit[None], piece, -1e30)
            return piece, line

        def sweep(size, step_at, state):
            state = lax.fori_loop(
                0, size // 32, lambda i, old: step_at(pl.multiple_of(i * 32, 32), 32, old), state,
                unroll=True,
            )
            return step_at(size - size % 32, size % 32, state) if size % 32 else state

        def add_tile(t, state):
            start, size = tiles[t]
            peak, total, weighted, chosen = state

            def widen(at, many, new):
                return jnp.maximum(new, jnp.max(part(t, start, at, many)[0], axis=0))

            new = sweep(size, widen, peak)
            move = peak - new
            factor = jnp.exp(move)
            weighted = factor * (weighted + total * move)
            total = factor * total

            def add(at, many, old):
                total, weighted, chosen = old
                piece, line = part(t, start, at, many)
                diff = piece - new[None]
                weights = jnp.exp(diff)
                total = total + jnp.sum(weights, axis=0)
                weighted = weighted + jnp.sum(weights * diff, axis=0)
                chosen = chosen + jnp.sum(jnp.where(line == target[None], piece, 0.0), axis=0)
                return total, weighted, chosen

            total, weighted, chosen = sweep(size, add, (total, weighted, chosen))
            return new, total, weighted, chosen

        zero = jnp.zeros((8, 2 * rows), jnp.float32)
        state = (zero - 1e30, zero, zero, zero)
        for t, (start, size) in enumerate(tiles):
            if t == len(tiles) // 2:
                pass_on(b, step, side)
            logits[t % 2, :size, :] = lax.dot_general(
                table[pl.ds(start, size), :], x, (((1,), (0,)), ((), ())),
                preferred_element_type=jnp.float32,
            )
            if t:
                state = add_tile(t - 1, state)
        peak, total, weighted, chosen = add_tile(len(tiles) - 1, state)
        top = jnp.max(peak, axis=0, keepdims=True)
        move = peak - top
        factor = jnp.exp(move)
        weighted = jnp.sum(factor * (weighted + total * move), axis=0, keepdims=True)
        total = jnp.sum(factor * total, axis=0, keepdims=True)
        chosen = jnp.sum(chosen, axis=0, keepdims=True)
        packed = jnp.concatenate([top, total, weighted, chosen, top, total, weighted, chosen], axis=0)
        fresh[place, 0] = packed[:, :rows]
        fresh[place, 1] = packed[:, rows:]

        for j in range(1, groups):
            stat_copy(b, place, 0, j).start()
            stat_copy(b, place, 1, j).start()

        @pl.when(b > 0)
        def _():
            stat_copy(b, place, 0, 0).start()
            stat_copy(b, place, 1, 0).start()

        @pl.when(b == 0)
        def _():
            stat_copy(b, place, 1 - c, 0).start()
            stats[0] = fresh[place, c]

        return carry

    lax.fori_loop(0, ring, block, 0)

    pltpu.make_async_remote_copy(
        src_ref=stats.at[others], dst_ref=stats.at[others], send_sem=ids_send.at[0],
        recv_sem=stat_recv, device_id=peer(1), device_id_type=MESH,
    ).wait_recv()

    for j in range(groups):
        peak = stats[j * n:(j + 1) * n, 0, :]
        total = stats[j * n:(j + 1) * n, 1, :]
        weighted = stats[j * n:(j + 1) * n, 2, :]
        chosen = jnp.sum(stats[j * n:(j + 1) * n, 3, :], axis=0, keepdims=True)
        top = jnp.max(peak, axis=0, keepdims=True)
        move = peak - top
        factor = jnp.exp(move)
        weighted = jnp.sum(factor * (weighted + total * move), axis=0, keepdims=True)
        total = jnp.sum(factor * total, axis=0, keepdims=True)
        log_total = jnp.log(total)
        out_ref[j] = jnp.concatenate([chosen - top - log_total, log_total - weighted / total], axis=0)

    def drain_ids(k, carry):
        ids_copy(k).wait_send()
        return carry

    lax.fori_loop(1, everyone, drain_ids, 0)

    def drain_ring(s, carry):
        chunk_copy(q, c, right_send.at[s], recv.at[q, c], right).wait_send()
        chunk_copy(q, c, left_send.at[s], recv.at[q, c], left).wait_send()
        return carry

    lax.fori_loop(0, last - 1, drain_ring, 0)
    chunk_copy(q, c, right_send.at[last - 1], recv.at[q, c], right, 0).wait_send()
    chunk_copy(q, c, left_send.at[last - 1], recv.at[q, c], left, 1).wait_send()

    def drain_block(b, carry):
        chunk_copy(q, c, sib_send.at[b], recv.at[q, c], sibling).wait_send()
        for j in range(1, groups):
            stat_copy(b, q, 0, j).wait_send()
            stat_copy(b, q, 1, j).wait_send()
        stat_copy(b, q, 1 - c, 0).wait_send()

        @pl.when(b > 0)
        def _():
            stat_copy(b, q, c, 0).wait_send()

        return carry

    lax.fori_loop(0, ring, drain_block, 0)


def local(groups, n, hidden, norm_gain, embedding, targets, lengths, loss_mask, deal_slots):
    seqs, width, depth = hidden.shape
    rows = seqs * width
    vocab = embedding.shape[0]
    ring = n // 2
    g = lax.axis_index("dp")
    r = lax.axis_index("tensor")
    every = jnp.arange(groups * seqs, dtype=jnp.int32)
    mine = g * seqs + jnp.arange(seqs, dtype=jnp.int32)
    order = jnp.sum(jnp.where(deal_slots[None, :] == mine[:, None], every[None, :], 0), axis=1)
    wanted = jnp.tile(targets, (1, seqs))
    tiles = vocab_tiles(vocab, 512)
    dma = pltpu.SemaphoreType.DMA
    result = pl.pallas_call(
        functools.partial(
            kernel, groups, n, seqs, tiles, VREAL - (n - 1) * vocab
        ),
        out_shape=jax.ShapeDtypeStruct((groups, 2, rows), jnp.float32),
        in_specs=[
            pl.BlockSpec(memory_space=pltpu.VMEM),
            pl.BlockSpec(memory_space=pltpu.VMEM),
            pl.BlockSpec(memory_space=pl.ANY),
            pl.BlockSpec(memory_space=pltpu.VMEM),
            pl.BlockSpec(memory_space=pltpu.SMEM),
        ],
        out_specs=pl.BlockSpec(memory_space=pltpu.VMEM),
        scratch_shapes=[
            pltpu.VMEM((ring, 2, rows, depth), jnp.bfloat16),
            pltpu.VMEM((vocab, depth), jnp.bfloat16),
            pltpu.VMEM((groups * n, seqs, rows), jnp.int32),
            pltpu.VMEM((ring, 2, 8, rows), jnp.float32),
            pltpu.VMEM((groups * n, 8, rows), jnp.float32),
            pltpu.VMEM((2, max(size for _, size in tiles), 2 * rows), jnp.float32),
            dma,
            dma((groups * n,)),
            dma,
            dma((ring // 2,)),
            dma((ring // 2,)),
            dma((ring,)),
            dma((ring, 2)),
            dma((2,)),
            dma((ring, 2, groups)),
            dma,
        ],
        compiler_params=pltpu.CompilerParams(
            collective_id=0, has_side_effects=True, vmem_limit_bytes=56 * 2**20
        ),
        cost_estimate=pl.CostEstimate(
            flops=2 * n * rows * vocab * depth,
            bytes_accessed=vocab * depth * 2,
            transcendentals=n * rows * vocab,
        ),
        name="ring_score",
    )(hidden.reshape(rows, depth), norm_gain, embedding, wanted, order)
    slots = lax.dynamic_slice_in_dim(deal_slots, g * seqs, seqs)
    back = lax.rem(g - slots // seqs + groups, groups)
    place = back * seqs + lax.rem(slots, seqs)
    pick = place[:, None] == jnp.arange(groups * seqs, dtype=jnp.int32)[None, :]
    flat = result.reshape(groups, 2, seqs, width).transpose(1, 0, 2, 3).reshape(2, groups * seqs, width)
    moved = jnp.sum(jnp.where(pick[None, :, :, None], flat[:, None], 0.0), axis=2)
    positions = r * width + jnp.arange(width, dtype=jnp.int32)
    scored = (positions[None, :] < lax.dynamic_slice_in_dim(lengths, g * seqs, seqs)[:, None]) & (loss_mask == 1)
    return jnp.where(scored, moved[0], 0.0), jnp.where(scored, moved[1], 0.0)


def solution(mesh):
    placed = (
        P("dp", "tensor", None),
        P(),
        P("tensor", None),
        P("dp", "tensor"),
        P(),
        P("dp", "tensor"),
        P(),
    )
    return jax.shard_map(
        functools.partial(local, mesh.shape["dp"], mesh.shape["tensor"]),
        mesh=mesh,
        in_specs=placed,
        out_specs=(P("dp", "tensor"), P("dp", "tensor")),
        check_vma=False,
    )
```
